32 devices in a mesh: grp: 4 (over y, core), blk: 8 (over z, x).
Axes of the slice: x: 2, y: 2, z: 4, core: 2. Of those that a mesh axis runs over, the one named last changes fastest.
Arguments:
- ratings: bfloat16 [8, 32768, 512], P(None, ('grp', 'blk')), may hold values from -6 to 6
- rated: int32 [8, 32768, 512], P(None, ('grp', 'blk')), may hold values 0 or 1
- user_factors: float32 [32768, 256], P(('grp', 'blk')), may hold values from -1.5 to 1.5
- item_ahead: bfloat16 [8192, 256], P(('grp', 'blk')), may hold values from -1.5 to 1.5
- item_behind: bfloat16 [8192, 256], P(('grp', 'blk')), may hold values from -1.5 to 1.5
- owners: int32 [2, 32], replicated, may hold values from 0 to 31, each once within a row
Outputs:
- user_out: float32 [32768, 256], P(('grp', 'blk'))
- ahead_out: bfloat16 [8192, 256], P(('grp', 'blk'))
- behind_out: bfloat16 [8192, 256], P(('grp', 'blk'))
The draws below stay inside these ranges and needn't reach their ends.
Inputs may be any that keep to these rules, and one draw needn't show every extreme that they name: `owners`: each row is a permutation of 0 .. 31.
All inputs are finite; a program needn't handle non-finite values. No bound on the sum of `rated` on one device may be relied on, other than what follows from the above.
Results may differ from the reference program's by a relative error of at most 0.0086.
Values may be sent and summed in bfloat16 or wider, within the bound.
A program may use at most 128 MiB of HBM per device.

```python
import jax
import jax.numpy as jnp

RANK = 256
HALF = 256
U_DEV = 1024
STRATA = 8
USERS = 32768
ITEMS_HALF = 8192
N_GRP = 4
N_BLK = 8
DEVICES = 32


def factor_draw(key, salt, rows):
    values = 0.25 * jax.random.normal(jax.random.fold_in(key, salt), (rows, RANK), jnp.float32)
    return jnp.clip(values, -1.5, 1.5)


def draw_user_factors(key, part):
    return factor_draw(key, 101, USERS).astype(jnp.float32)


def draw_item_ahead(key, part):
    return factor_draw(key, 202, ITEMS_HALF).astype(jnp.bfloat16)


def draw_item_behind(key, part):
    return factor_draw(key, 303, ITEMS_HALF).astype(jnp.bfloat16)


def plant(entries, key, low, top_value):
    longest = entries.shape.index(max(entries.shape))
    spots = []
    for shift in (0, 1):
        where = [jax.random.randint(jax.random.fold_in(key, axis), (), 0, length) for axis, length in enumerate(entries.shape)]
        where[longest] = (where[longest] + shift) % entries.shape[longest]
        spots.append(tuple(where))
    return entries.at[spots[0]].set(low).at[spots[1]].set(top_value)


def shard_levels(stream_key, extent, pieces, smallest, top_value):
    def one(dim, parts):
        heights = jax.random.uniform(jax.random.fold_in(jax.random.fold_in(stream_key, 6), dim), (parts,), jnp.float32, smallest / len(pieces), top_value / len(pieces))
        return jnp.repeat(jnp.exp(heights), extent[dim] // parts).reshape((-1,) + (1,) * (len(extent) - dim - 1))

    gain = one(*pieces[0])
    for cut in pieces[1:]:
        gain = gain * one(*cut)
    return gain


def bell_draw(own_key, extent, deviation, bound, split=(), held_as=jnp.bfloat16):
    entries = jax.random.normal(own_key, extent, jnp.float32) * deviation
    if len(split) > 0:
        entries = shard_levels(own_key, extent, split, -0.22, 0.18) * entries
    return jnp.clip(entries, min=-bound, max=bound).astype(held_as)


def setup_inputs(seed: int = 0) -> dict:
    splits = jax.random.split(jax.random.key(seed), 7)
    ratings = bell_draw(splits[0], (STRATA, USERS, 2 * HALF), 1.0, 6.0, ((1, 32),))
    rated = plant((jax.random.randint(splits[1], (STRATA, USERS, 2 * HALF), 0, 2) < 1).astype(jnp.int32), jax.random.fold_in(splits[1], 1), 0, 1)
    user_factors = draw_user_factors(jax.random.fold_in(splits[6], 71), 0)
    item_ahead = draw_item_ahead(jax.random.fold_in(splits[6], 71), 0)
    item_behind = draw_item_behind(jax.random.fold_in(splits[6], 71), 0)
    owners = jax.vmap(lambda own: jax.random.permutation(own, DEVICES))(jax.random.split(splits[5], 2)).reshape((2, DEVICES)).astype(jnp.int32)
    return dict(ratings=ratings, rated=rated, user_factors=user_factors, item_ahead=item_ahead, item_behind=item_behind, owners=owners)


RATE = 0.005
DECAY = 0.05


def reference(ratings, rated, user_factors, item_ahead, item_behind, owners):
    count = N_GRP * N_BLK
    users = user_factors.reshape(count, U_DEV, RANK)
    ahead = item_ahead.reshape(count, HALF, RANK)
    behind = item_behind.reshape(count, HALF, RANK)
    for stratum in range(STRATA):
        if stratum == STRATA // 2:
            ahead = jnp.zeros_like(ahead).at[owners[0]].set(ahead)
            behind = jnp.zeros_like(behind).at[owners[1]].set(behind)
        block = jnp.concatenate([ahead, behind], axis=1)
        block_f = block.astype(jnp.float32)
        user_b = users.astype(jnp.bfloat16).astype(jnp.float32)
        pred = jnp.einsum('nur,nir->nui', user_b, block_f)
        target = ratings[stratum].reshape(count, U_DEV, 2 * HALF).astype(jnp.float32)
        mask = rated[stratum].reshape(count, U_DEV, 2 * HALF)
        err = jnp.where(mask == 1, pred - target, 0.0).astype(jnp.bfloat16).astype(jnp.float32)
        grad_user = jnp.einsum('nui,nir->nur', err, block_f)
        grad_item = jnp.einsum('nui,nur->nir', err, user_b)
        users = users - RATE * (grad_user + DECAY * users)
        block = (block_f - RATE * (grad_item + DECAY * block_f)).astype(jnp.bfloat16)
        ahead = block[:, :HALF]
        behind = block[:, HALF:]
        if stratum < STRATA - 1:
            ahead = jnp.roll(ahead, 1, axis=0)
            behind = jnp.roll(behind, -1, axis=0)
    return (users.reshape(count * U_DEV, RANK),
            ahead.reshape(count * HALF, RANK),
            behind.reshape(count * HALF, RANK))
```

```python
import functools

import jax
import jax.numpy as jnp
from jax import lax
from jax.experimental import pallas as pl
from jax.experimental.pallas import tpu as pltpu
from jax.sharding import PartitionSpec as P

RATE = 0.005
DECAY = 0.05
TABLES = 2
PARTS = 4
MESH = pl.DeviceIdType.MESH


def line_split(columns):
    inner = 1
    while columns % (inner * inner * 4) == 0 or (columns % (inner * 2) == 0 and inner * inner * 4 <= columns):
        inner *= 2
    return columns // inner, inner


def kernel(
    groups, columns, strata,
    ratings, rated, users_in, ahead_in, behind_in, owners,
    users, ahead_out, behind_out,
    rate_buf, mask_buf, q_in, q_out, user_b, err,
    *rest,
):
    gath = rest[:PARTS]
    outb = rest[PARTS:2 * PARTS]
    fin = rest[2 * PARTS:3 * PARTS]
    (rate_sem, mask_sem, ring_send, ring_recv, core_send, core_recv,
     line_send, line_recv, all_send, all_recv) = rest[3 * PARTS:]

    count = groups * columns
    line, inner = line_split(columns)
    pairs = groups // TABLES
    mid = strata // 2
    half = ahead_in.shape[0]
    rows = half // PARTS

    g = lax.axis_index("grp")
    b = lax.axis_index("blk")
    me = g * columns + b
    c = lax.rem(g, TABLES)
    y = lax.div(g, TABLES)
    z = lax.div(b, inner)
    x = lax.rem(b, inner)

    def load_rate(s):
        return pltpu.make_async_copy(ratings.at[s], rate_buf.at[s], rate_sem.at[s])

    def load_mask(s):
        return pltpu.make_async_copy(rated.at[s], mask_buf.at[s], mask_sem.at[s])

    def at(d):
        return (lax.div(d, columns), lax.rem(d, columns))

    after = at(lax.rem(me + 1, count))
    before = at(lax.rem(me + count - 1, count))
    mate = (y * TABLES + (TABLES - 1 - c), b)
    up = (g, jnp.minimum(z + 1, line - 1) * inner + x)
    down = (g, jnp.maximum(z - 1, 0) * inner + x)
    offsets = [
        (dy, dx, dc)
        for dy in range(pairs) for dx in range(inner) for dc in range(TABLES)
        if (dy, dx, dc) != (0, 0, 0)
    ]

    def peer(dy, dx, dc):
        return (
            lax.rem(y + dy, pairs) * TABLES + lax.rem(c + dc, TABLES),
            z * inner + lax.rem(x + dx, inner),
        )

    barrier = pltpu.get_barrier_semaphore()

    def greet(device):
        pl.semaphore_signal(barrier, inc=1, device_id=device, device_id_type=MESH)

    greet(after)
    greet(before)
    for o in offsets:
        greet(peer(*o))

    @pl.when(z + 1 < line)
    def _():
        greet(up)

    @pl.when(z > 0)
    def _():
        greet(down)

    def issue(s, carry):
        load_rate(s).start()
        load_mask(s).start()
        return carry

    lax.fori_loop(0, strata, issue, 0)

    q_in[0, 0] = ahead_in[...]
    q_in[0, 1] = behind_in[...]
    users[...] = users_in[...]
    user_b[...] = users_in[...].astype(jnp.bfloat16)

    greeted = 2 + len(offsets)
    greeted = greeted + jnp.where(z + 1 < line, 1, 0) + jnp.where(z > 0, 1, 0)
    pl.semaphore_wait(barrier, greeted)

    def ring(s, t):
        return pltpu.make_async_remote_copy(
            src_ref=q_out.at[s, t], dst_ref=q_in.at[s + 1, t],
            send_sem=ring_send.at[s, t], recv_sem=ring_recv.at[s + 1, t],
            device_id=after if t == 0 else before, device_id_type=MESH,
        )

    def ring_arrival(s, t):
        return pltpu.make_async_remote_copy(
            src_ref=q_out.at[s, t], dst_ref=q_in.at[s, t],
            send_sem=ring_send.at[s, t], recv_sem=ring_recv.at[s, t],
            device_id=after if t == 0 else before, device_id_type=MESH,
        )

    own = z * TABLES + c

    def mate_copy(p):
        return pltpu.make_async_remote_copy(
            src_ref=q_out.at[mid - 1, TABLES - 1 - c, pl.ds(p * rows, rows)],
            dst_ref=gath[p].at[own],
            send_sem=core_send.at[p], recv_sem=core_recv.at[p],
            device_id=mate, device_id_type=MESH,
        )

    def line_copy(p, k, way):
        src = z - k if way == 0 else z + k
        slot = gath[p].at[pl.ds(src * TABLES, TABLES)]
        return pltpu.make_async_remote_copy(
            src_ref=slot, dst_ref=slot,
            send_sem=line_send.at[p, k, way], recv_sem=line_recv.at[p, k, way],
            device_id=up if way == 0 else down, device_id_type=MESH,
        )

    def line_sends(k, way):
        if way == 0:
            return jnp.logical_and(z - k >= 0, z + 1 < line)
        return jnp.logical_and(z + k < line, z > 0)

    def line_arrival(p, k, way):
        src = z - k - 1 if way == 0 else z + k + 1
        slot = gath[p].at[pl.ds(src * TABLES, TABLES)]
        return pltpu.make_async_remote_copy(
            src_ref=slot, dst_ref=slot,
            send_sem=line_send.at[p, k, way], recv_sem=line_recv.at[p, k, way],
            device_id=up if way == 0 else down, device_id_type=MESH,
        )

    def line_gets(k, way):
        return z - k - 1 >= 0 if way == 0 else z + k + 1 < line

    chips = pairs * inner
    chip = y * inner + x

    def all_copy(p, i):
        return pltpu.make_async_remote_copy(
            src_ref=outb[p].at[i], dst_ref=fin[p].at[c * chips + chip],
            send_sem=all_send.at[p, i], recv_sem=all_recv.at[p, i],
            device_id=peer(*offsets[i]), device_id_type=MESH,
        )

    def all_arrival(p, i):
        dy, dx, dc = offsets[i]
        source = lax.rem(y + pairs - dy, pairs) * inner + lax.rem(x + inner - dx, inner)
        return pltpu.make_async_remote_copy(
            src_ref=outb[p].at[i],
            dst_ref=fin[p].at[lax.rem(c + TABLES - dc, TABLES) * chips + source],
            send_sem=all_send.at[p, i], recv_sem=all_recv.at[p, i],
            device_id=peer(*offsets[i]), device_id_type=MESH,
        )

    def exchange():
        for p in range(PARTS):
            mate_copy(p).start()
            gath[p][own] = q_out[mid - 1, c, pl.ds(p * rows, rows)]
        step = jnp.where(c == 0, 1, count - 1)
        holders = []
        for zs in range(line):
            for cs in range(TABLES):
                src = (y * TABLES + cs) * columns + zs * inner + x
                holders.append(owners[c, lax.rem(src + step, count)])

        def pick(device):
            target = device[0] * columns + device[1]
            j = jnp.int32(0)
            for k, holder in enumerate(holders):
                j = jnp.where(holder == target, k, j)
            return j

        picks = [pick(peer(*o)) for o in offsets]
        self_pick = pick((g, b))
        origin = []
        for t in range(TABLES):
            found = jnp.int32(0)
            for src in range(count):
                sg, sb = divmod(src, columns)
                shifted = (src + (1 if t == 0 else count - 1)) % count
                found = jnp.where(
                    owners[t, shifted] == me, (sg // TABLES) * inner + sb % inner, found
                )
            origin.append(t * chips + found)

        def advance(p, k):
            if k == 0:
                arrived = pltpu.make_async_remote_copy(
                    src_ref=q_out.at[mid - 1, TABLES - 1 - c, pl.ds(p * rows, rows)],
                    dst_ref=gath[p].at[z * TABLES + (TABLES - 1 - c)],
                    send_sem=core_send.at[p], recv_sem=core_recv.at[p],
                    device_id=mate, device_id_type=MESH,
                )
                arrived.wait_recv()
            else:
                for way in range(2):
                    @pl.when(line_gets(k - 1, way))
                    def _():
                        line_arrival(p, k - 1, way).wait_recv()
            if k < line - 1:
                for way in range(2):
                    @pl.when(line_sends(k, way))
                    def _():
                        line_copy(p, k, way).start()
            else:
                for i in range(len(offsets)):
                    outb[p][i] = gath[p][picks[i]]
                    all_copy(p, i).start()
                fin[p][c * chips + chip] = gath[p][self_pick]

        for wave in range(PARTS + line - 1):
            for p in range(PARTS):
                if 0 <= wave - p < line:
                    advance(p, wave - p)
        for p in range(PARTS):
            for i in range(len(offsets)):
                all_arrival(p, i).wait_recv()
            for t in range(TABLES):
                q_in[mid, t, pl.ds(p * rows, rows)] = fin[p][origin[t]]
        for p in range(PARTS):
            mate_copy(p).wait_send()
            for k in range(line - 1):
                for way in range(2):
                    @pl.when(line_sends(k, way))
                    def _():
                        line_copy(p, k, way).wait_send()
            for i in range(len(offsets)):
                all_copy(p, i).wait_send()

    def stratum(s, carry):
        @pl.when(s == mid)
        def _():
            exchange()

        load_rate(s).wait()
        load_mask(s).wait()
        for t in range(TABLES):
            @pl.when(jnp.logical_and(s > 0, s != mid))
            def _():
                ring_arrival(s, t).wait_recv()

            block = q_in[s, t]
            part = slice(t * half, (t + 1) * half)
            pred = lax.dot_general(
                user_b[...], block, (((1,), (1,)), ((), ())),
                preferred_element_type=jnp.float32,
            )
            err[:, part] = jnp.where(
                mask_buf[s, :, part] == 1,
                pred - rate_buf[s, :, part].astype(jnp.float32), 0.0,
            ).astype(jnp.bfloat16)
            grad_item = lax.dot_general(
                err[:, part], user_b[...], (((0,), (0,)), ((), ())),
                preferred_element_type=jnp.float32,
            )
            block_f = block.astype(jnp.float32)
            q_out[s, t] = (
                block_f - RATE * (grad_item + DECAY * block_f)
            ).astype(jnp.bfloat16)

            @pl.when(jnp.logical_and(s < strata - 1, s != mid - 1))
            def _():
                ring(s, t).start()

        grad_user = jnp.dot(
            err[...], q_in[s].reshape(TABLES * half, -1), preferred_element_type=jnp.float32
        )
        old = users[...]
        new = old - RATE * (grad_user + DECAY * old)
        users[...] = new
        user_b[...] = new.astype(jnp.bfloat16)
        return carry

    lax.fori_loop(0, strata, stratum, 0)
    ahead_out[...] = q_out[strata - 1, 0]
    behind_out[...] = q_out[strata - 1, 1]

    def drain(s, carry):
        @pl.when(s != mid - 1)
        def _():
            for t in range(TABLES):
                ring(s, t).wait_send()
        return carry

    lax.fori_loop(0, strata - 1, drain, 0)


def body(ratings, rated, user_factors, item_ahead, item_behind, owners):
    groups = lax.axis_size("grp")
    columns = lax.axis_size("blk")
    strata, own_users, items = ratings.shape
    half, rank = item_ahead.shape
    rows = half // PARTS
    line, inner = line_split(columns)
    chips = (groups // TABLES) * inner
    peers = chips * TABLES - 1
    vmem = pl.BlockSpec(memory_space=pltpu.VMEM)
    anywhere = pl.BlockSpec(memory_space=pl.ANY)
    bf16 = jnp.bfloat16
    dma = pltpu.SemaphoreType.DMA
    scratch = (
        [
            pltpu.VMEM((strata, own_users, items), ratings.dtype),
            pltpu.VMEM((strata, own_users, items), rated.dtype),
            pltpu.VMEM((strata, TABLES, half, rank), bf16),
            pltpu.VMEM((strata, TABLES, half, rank), bf16),
            pltpu.VMEM((own_users, rank), bf16),
            pltpu.VMEM((own_users, items), bf16),
        ]
        + [pltpu.VMEM((line * TABLES, rows, rank), bf16)] * PARTS
        + [pltpu.VMEM((peers, rows, rank), bf16)] * PARTS
        + [pltpu.VMEM((TABLES * chips, rows, rank), bf16)] * PARTS
        + [
            dma((strata,)), dma((strata,)),
            dma((strata, TABLES)), dma((strata, TABLES)),
            dma((PARTS,)), dma((PARTS,)),
            dma((PARTS, line - 1, 2)), dma((PARTS, line - 1, 2)),
            dma((PARTS, peers)), dma((PARTS, peers)),
        ]
    )
    return pl.pallas_call(
        functools.partial(kernel, groups, columns, strata),
        out_shape=(
            jax.ShapeDtypeStruct(user_factors.shape, jnp.float32),
            jax.ShapeDtypeStruct(item_ahead.shape, bf16),
            jax.ShapeDtypeStruct(item_behind.shape, bf16),
        ),
        in_specs=[anywhere, anywhere, vmem, vmem, vmem,
                  pl.BlockSpec(memory_space=pltpu.SMEM)],
        out_specs=(vmem, vmem, vmem),
        scratch_shapes=scratch,
        compiler_params=pltpu.CompilerParams(
            collective_id=0, has_side_effects=True, vmem_limit_bytes=56 * 1024 * 1024
        ),
        cost_estimate=pl.CostEstimate(
            flops=6 * strata * own_users * items * rank,
            bytes_accessed=6 * strata * own_users * items, transcendentals=0,
        ),
    )(ratings, rated, user_factors, item_ahead, item_behind, owners)


def solution(mesh):
    shard = P(("grp", "blk"), None)
    strata = P(None, ("grp", "blk"), None)
    return jax.shard_map(
        body, mesh=mesh,
        in_specs=(strata, strata, shard, shard, shard, P()),
        out_specs=(shard, shard, shard), check_vma=False,
    )
```

```python
import functools

import jax
import jax.numpy as jnp
from jax import lax
from jax.experimental import pallas as pl
from jax.experimental.pallas import tpu as pltpu
from jax.sharding import PartitionSpec as P

RATE = 0.005
DECAY = 0.05
TABLES = 2
AHEAD = 2
SPLIT = 2
PARTS = 2
MESH = pl.DeviceIdType.MESH


def line_split(columns):
    inner = 1
    while columns % (inner * inner * 4) == 0 or (columns % (inner * 2) == 0 and inner * inner * 4 <= columns):
        inner *= 2
    return columns // inner, inner


def kernel(
    groups, columns, strata,
    ratings, rated, users_in, ahead_in, behind_in, owners,
    users, ahead_out, behind_out,
    rate_buf, mask_buf, q_in, q_out, user_b, err, total,
    *rest,
):
    gath = rest[:PARTS]
    outb = rest[PARTS:2 * PARTS]
    fin = rest[2 * PARTS:3 * PARTS]
    (rate_sem, mask_sem, ring_send, ring_recv, core_send, core_recv,
     line_send, line_recv, all_send, all_recv) = rest[3 * PARTS:]

    count = groups * columns
    line, inner = line_split(columns)
    pairs = groups // TABLES
    mid = strata // 2
    half = ahead_in.shape[0]
    rows = half // PARTS

    g = lax.axis_index("grp")
    b = lax.axis_index("blk")
    me = g * columns + b
    c = lax.rem(g, TABLES)
    y = lax.div(g, TABLES)
    z = lax.div(b, inner)
    x = lax.rem(b, inner)

    def load_rate(s):
        return pltpu.make_async_copy(ratings.at[s], rate_buf.at[s], rate_sem.at[s])

    def load_mask(s):
        return pltpu.make_async_copy(rated.at[s], mask_buf.at[s], mask_sem.at[s])

    def at(d):
        return (lax.div(d, columns), lax.rem(d, columns))

    after = at(lax.rem(me + 1, count))
    before = at(lax.rem(me + count - 1, count))
    mate = (y * TABLES + (TABLES - 1 - c), b)
    up = (g, jnp.minimum(z + 1, line - 1) * inner + x)
    down = (g, jnp.maximum(z - 1, 0) * inner + x)
    offsets = [
        (dy, dx, dc)
        for dy in range(pairs) for dx in range(inner) for dc in range(TABLES)
        if (dy, dx, dc) != (0, 0, 0)
    ]

    def peer(dy, dx, dc):
        return (
            lax.rem(y + dy, pairs) * TABLES + lax.rem(c + dc, TABLES),
            z * inner + lax.rem(x + dx, inner),
        )

    barrier = pltpu.get_barrier_semaphore()

    def greet(device):
        pl.semaphore_signal(barrier, inc=1, device_id=device, device_id_type=MESH)

    greet(after)
    greet(before)
    for o in offsets:
        greet(peer(*o))

    @pl.when(z + 1 < line)
    def _():
        greet(up)

    @pl.when(z > 0)
    def _():
        greet(down)

    def issue(s):
        load_rate(s).start()
        load_mask(s).start()

    early = min(AHEAD, strata)
    for s in range(early):
        issue(s)

    q_in[0, 0] = ahead_in[...]
    q_in[0, 1] = behind_in[...]
    users[...] = users_in[...]
    user_b[...] = users_in[...].astype(jnp.bfloat16)

    greeted = 2 + len(offsets)
    greeted = greeted + jnp.where(z + 1 < line, 1, 0) + jnp.where(z > 0, 1, 0)

    piece = half // SPLIT

    def ring(s, t, i):
        span = pl.ds(i * piece, piece)
        return pltpu.make_async_remote_copy(
            src_ref=q_out.at[s, t, span], dst_ref=q_in.at[s + 1, t, span],
            send_sem=ring_send.at[s, t, i], recv_sem=ring_recv.at[s + 1, t, i],
            device_id=after if t == 0 else before, device_id_type=MESH,
        )

    def ring_arrival(s, t, i):
        span = pl.ds(i * piece, piece)
        return pltpu.make_async_remote_copy(
            src_ref=q_out.at[s, t, span], dst_ref=q_in.at[s, t, span],
            send_sem=ring_send.at[s, t, i], recv_sem=ring_recv.at[s, t, i],
            device_id=after if t == 0 else before, device_id_type=MESH,
        )

    own = z * TABLES + c

    def mate_copy(p):
        return pltpu.make_async_remote_copy(
            src_ref=q_out.at[mid - 1, TABLES - 1 - c, pl.ds(p * rows, rows)],
            dst_ref=gath[p].at[own],
            send_sem=core_send.at[p], recv_sem=core_recv.at[p],
            device_id=mate, device_id_type=MESH,
        )

    def line_copy(p, k, way):
        src = z - k if way == 0 else z + k
        slot = gath[p].at[pl.ds(src * TABLES, TABLES)]
        return pltpu.make_async_remote_copy(
            src_ref=slot, dst_ref=slot,
            send_sem=line_send.at[p, k, way], recv_sem=line_recv.at[p, k, way],
            device_id=up if way == 0 else down, device_id_type=MESH,
        )

    def line_sends(k, way):
        if way == 0:
            return jnp.logical_and(z - k >= 0, z + 1 < line)
        return jnp.logical_and(z + k < line, z > 0)

    def line_arrival(p, k, way):
        src = z - k - 1 if way == 0 else z + k + 1
        slot = gath[p].at[pl.ds(src * TABLES, TABLES)]
        return pltpu.make_async_remote_copy(
            src_ref=slot, dst_ref=slot,
            send_sem=line_send.at[p, k, way], recv_sem=line_recv.at[p, k, way],
            device_id=up if way == 0 else down, device_id_type=MESH,
        )

    def line_gets(k, way):
        return z - k - 1 >= 0 if way == 0 else z + k + 1 < line

    chips = pairs * inner
    chip = y * inner + x

    def all_copy(p, i):
        return pltpu.make_async_remote_copy(
            src_ref=outb[p].at[i], dst_ref=fin[p].at[c * chips + chip],
            send_sem=all_send.at[p, i], recv_sem=all_recv.at[p, i],
            device_id=peer(*offsets[i]), device_id_type=MESH,
        )

    def all_arrival(p, i):
        dy, dx, dc = offsets[i]
        source = lax.rem(y + pairs - dy, pairs) * inner + lax.rem(x + inner - dx, inner)
        return pltpu.make_async_remote_copy(
            src_ref=outb[p].at[i],
            dst_ref=fin[p].at[lax.rem(c + TABLES - dc, TABLES) * chips + source],
            send_sem=all_send.at[p, i], recv_sem=all_recv.at[p, i],
            device_id=peer(*offsets[i]), device_id_type=MESH,
        )

    def exchange_start():
        for p in range(PARTS):
            mate_copy(p).start()
            gath[p][own] = q_out[mid - 1, c, pl.ds(p * rows, rows)]

    def exchange():
        step = jnp.where(c == 0, 1, count - 1)
        holders = []
        for zs in range(line):
            for cs in range(TABLES):
                src = (y * TABLES + cs) * columns + zs * inner + x
                holders.append(owners[c, lax.rem(src + step, count)])

        def pick(device):
            target = device[0] * columns + device[1]
            j = jnp.int32(0)
            for k, holder in enumerate(holders):
                j = jnp.where(holder == target, k, j)
            return j

        picks = [pick(peer(*o)) for o in offsets]
        self_pick = pick((g, b))
        origin = []
        for t in range(TABLES):
            found = jnp.int32(0)
            for src in range(count):
                sg, sb = divmod(src, columns)
                shifted = (src + (1 if t == 0 else count - 1)) % count
                found = jnp.where(
                    owners[t, shifted] == me, (sg // TABLES) * inner + sb % inner, found
                )
            origin.append(t * chips + found)

        def advance(p, k):
            if k == 0:
                arrived = pltpu.make_async_remote_copy(
                    src_ref=q_out.at[mid - 1, TABLES - 1 - c, pl.ds(p * rows, rows)],
                    dst_ref=gath[p].at[z * TABLES + (TABLES - 1 - c)],
                    send_sem=core_send.at[p], recv_sem=core_recv.at[p],
                    device_id=mate, device_id_type=MESH,
                )
                arrived.wait_recv()
            else:
                for way in range(2):
                    @pl.when(line_gets(k - 1, way))
                    def _():
                        line_arrival(p, k - 1, way).wait_recv()
            if k < line - 1:
                for way in range(2):
                    @pl.when(line_sends(k, way))
                    def _():
                        line_copy(p, k, way).start()
            else:
                for i in range(len(offsets)):
                    outb[p][i] = gath[p][picks[i]]
                    all_copy(p, i).start()
                fin[p][c * chips + chip] = gath[p][self_pick]

        for wave in range(PARTS + line - 1):
            for p in range(PARTS):
                if 0 <= wave - p < line:
                    advance(p, wave - p)
        for p in range(PARTS):
            for i in range(len(offsets)):
                all_arrival(p, i).wait_recv()
            for t in range(TABLES):
                q_in[mid, t, pl.ds(p * rows, rows)] = fin[p][origin[t]]
        for p in range(PARTS):
            mate_copy(p).wait_send()
            for k in range(line - 1):
                for way in range(2):
                    @pl.when(line_sends(k, way))
                    def _():
                        line_copy(p, k, way).wait_send()
            for i in range(len(offsets)):
                all_copy(p, i).wait_send()

    pieces = [(i, t) for i in range(SPLIT) for t in range(TABLES)]

    def stratum(s, carry):
        load_rate(s).wait()
        load_mask(s).wait()

        @pl.when(s + early < strata)
        def _():
            issue(s + early)

        for k, (i, t) in enumerate(pieces):
            @pl.when(jnp.logical_and(s > 0, s != mid))
            def _():
                ring_arrival(s, t, i).wait_recv()

            span = slice(i * piece, (i + 1) * piece)
            part = slice(t * half + i * piece, t * half + (i + 1) * piece)
            block = q_in[s, t, span]
            pred = lax.dot_general(
                user_b[...], block, (((1,), (1,)), ((), ())),
                preferred_element_type=jnp.float32,
            )
            err[:, part] = jnp.where(
                mask_buf[s, :, part] == 1,
                pred - rate_buf[s, :, part].astype(jnp.float32), 0.0,
            ).astype(jnp.bfloat16)
            grad_item = lax.dot_general(
                err[:, part], user_b[...], (((0,), (0,)), ((), ())),
                preferred_element_type=jnp.float32,
            )
            block_f = block.astype(jnp.float32)
            q_out[s, t, span] = (
                block_f - RATE * (grad_item + DECAY * block_f)
            ).astype(jnp.bfloat16)

            if k == 0:
                @pl.when(s == 0)
                def _():
                    pl.semaphore_wait(barrier, greeted)

            @pl.when(jnp.logical_and(s < strata - 1, s != mid - 1))
            def _():
                ring(s, t, i).start()

            if k == len(pieces) - 1:
                @pl.when(s == mid - 1)
                def _():
                    exchange_start()

            grad_user = jnp.dot(err[:, part], block, preferred_element_type=jnp.float32)
            if k == 0:
                total[...] = grad_user
            elif k < len(pieces) - 1:
                total[...] += grad_user
            else:
                old = users[...]
                new = old - RATE * (total[...] + grad_user + DECAY * old)
                users[...] = new
                user_b[...] = new.astype(jnp.bfloat16)

        @pl.when(s == mid - 1)
        def _():
            exchange()

        return carry

    lax.fori_loop(0, strata, stratum, 0)
    ahead_out[...] = q_out[strata - 1, 0]
    behind_out[...] = q_out[strata - 1, 1]

    def drain(s, carry):
        @pl.when(s != mid - 1)
        def _():
            for i, t in pieces:
                ring(s, t, i).wait_send()
        return carry

    lax.fori_loop(0, strata - 1, drain, 0)


def settle(arrays):
    shapes = tuple(jax.ShapeDtypeStruct(a.shape, a.dtype) for a in arrays)
    n = len(arrays)
    where = pl.BlockSpec(memory_space=pltpu.VMEM)

    def copies(*refs):
        for i in range(n):
            refs[n + i][...] = refs[i][...]

    return pl.pallas_call(
        copies, out_shape=shapes, in_specs=[where] * n, out_specs=(where,) * n,
    )(*arrays)


def body(ratings, rated, user_factors, item_ahead, item_behind, owners):
    groups = lax.axis_size("grp")
    columns = lax.axis_size("blk")
    strata, own_users, items = ratings.shape
    half, rank = item_ahead.shape
    rows = half // PARTS
    line, inner = line_split(columns)
    chips = (groups // TABLES) * inner
    peers = chips * TABLES - 1
    vmem = pl.BlockSpec(memory_space=pltpu.VMEM)
    anywhere = pl.BlockSpec(memory_space=pl.ANY)
    bf16 = jnp.bfloat16
    dma = pltpu.SemaphoreType.DMA
    scratch = (
        [
            pltpu.VMEM((strata, own_users, items), ratings.dtype),
            pltpu.VMEM((strata, own_users, items), rated.dtype),
            pltpu.VMEM((strata, TABLES, half, rank), bf16),
            pltpu.VMEM((strata, TABLES, half, rank), bf16),
            pltpu.VMEM((own_users, rank), bf16),
            pltpu.VMEM((own_users, items), bf16),
            pltpu.VMEM((own_users, rank), jnp.float32),
        ]
        + [pltpu.VMEM((line * TABLES, rows, rank), bf16)] * PARTS
        + [pltpu.VMEM((peers, rows, rank), bf16)] * PARTS
        + [pltpu.VMEM((TABLES * chips, rows, rank), bf16)] * PARTS
        + [
            dma((strata,)), dma((strata,)),
            dma((strata, TABLES, SPLIT)), dma((strata, TABLES, SPLIT)),
            dma((PARTS,)), dma((PARTS,)),
            dma((PARTS, line - 1, 2)), dma((PARTS, line - 1, 2)),
            dma((PARTS, peers)), dma((PARTS, peers)),
        ]
    )
    moved = pl.pallas_call(
        functools.partial(kernel, groups, columns, strata),
        out_shape=(
            jax.ShapeDtypeStruct(user_factors.shape, jnp.float32),
            jax.ShapeDtypeStruct(item_ahead.shape, bf16),
            jax.ShapeDtypeStruct(item_behind.shape, bf16),
        ),
        in_specs=[anywhere, anywhere, vmem, vmem, vmem,
                  pl.BlockSpec(memory_space=pltpu.SMEM)],
        out_specs=(vmem, vmem, vmem),
        scratch_shapes=scratch,
        compiler_params=pltpu.CompilerParams(
            collective_id=0, has_side_effects=True, vmem_limit_bytes=56 * 1024 * 1024
        ),
        cost_estimate=pl.CostEstimate(
            flops=6 * strata * own_users * items * rank,
            bytes_accessed=6 * strata * own_users * items, transcendentals=0,
        ),
    )(ratings, rated, user_factors, item_ahead, item_behind, owners)
    return settle(moved)


def solution(mesh):
    shard = P(("grp", "blk"), None)
    strata = P(None, ("grp", "blk"), None)
    return jax.shard_map(
        body, mesh=mesh,
        in_specs=(strata, strata, shard, shard, shard, P()),
        out_specs=(shard, shard, shard), check_vma=False,
    )
```

```python
import functools

import jax
import jax.numpy as jnp
from jax import lax
from jax.experimental import pallas as pl
from jax.experimental.pallas import tpu as pltpu
from jax.sharding import PartitionSpec as P

RATE = 0.005
DECAY = 0.05
TABLES = 2
AHEAD = 2
SPLIT = 2
PARTS = 2
MESH = pl.DeviceIdType.MESH


def line_split(columns):
    inner = 1
    while columns % (inner * inner * 4) == 0 or (columns % (inner * 2) == 0 and inner * inner * 4 <= columns):
        inner *= 2
    return columns // inner, inner


def kernel(
    groups, columns, strata,
    ratings, rated, users_in, ahead_in, behind_in, owners,
    users, ahead_out, behind_out,
    rate_buf, mask_buf, q_in, q_out, user_b, err, total,
    *rest,
):
    gath = rest[:PARTS]
    outb = rest[PARTS:2 * PARTS]
    fin = rest[2 * PARTS:3 * PARTS]
    (rate_sem, mask_sem, ring_send, ring_recv, core_send, core_recv,
     line_send, line_recv, lead_send, lead_recv, all_send, all_recv) = rest[3 * PARTS:]

    count = groups * columns
    line, inner = line_split(columns)
    pairs = groups // TABLES
    mid = strata // 2
    half = ahead_in.shape[0]
    rows = half // PARTS

    g = lax.axis_index("grp")
    b = lax.axis_index("blk")
    me = g * columns + b
    c = lax.rem(g, TABLES)
    y = lax.div(g, TABLES)
    z = lax.div(b, inner)
    x = lax.rem(b, inner)

    def load_rate(s):
        return pltpu.make_async_copy(ratings.at[s], rate_buf.at[s], rate_sem.at[s])

    def load_mask(s):
        return pltpu.make_async_copy(rated.at[s], mask_buf.at[s], mask_sem.at[s])

    def at(d):
        return (lax.div(d, columns), lax.rem(d, columns))

    after = at(lax.rem(me + 1, count))
    before = at(lax.rem(me + count - 1, count))
    mate = (y * TABLES + (TABLES - 1 - c), b)
    up = (g, jnp.minimum(z + 1, line - 1) * inner + x)
    down = (g, jnp.maximum(z - 1, 0) * inner + x)
    offsets = [
        (dy, dx, dc)
        for dy in range(pairs) for dx in range(inner) for dc in range(TABLES)
        if (dy, dx, dc) != (0, 0, 0)
    ]

    def peer(dy, dx, dc):
        return (
            lax.rem(y + dy, pairs) * TABLES + lax.rem(c + dc, TABLES),
            z * inner + lax.rem(x + dx, inner),
        )

    barrier = pltpu.get_barrier_semaphore()

    def greet(device):
        pl.semaphore_signal(barrier, inc=1, device_id=device, device_id_type=MESH)

    greet(after)
    greet(before)
    for o in offsets:
        greet(peer(*o))

    @pl.when(z + 1 < line)
    def _():
        greet(up)

    @pl.when(z > 0)
    def _():
        greet(down)

    def issue(s):
        load_rate(s).start()
        load_mask(s).start()

    early = min(AHEAD, strata)
    for s in range(early):
        issue(s)

    q_in[0, 0] = ahead_in[...]
    q_in[0, 1] = behind_in[...]
    users[...] = users_in[...]
    user_b[...] = users_in[...].astype(jnp.bfloat16)

    greeted = 2 + len(offsets)
    greeted = greeted + jnp.where(z + 1 < line, 1, 0) + jnp.where(z > 0, 1, 0)

    piece = half // SPLIT

    def ring(s, t, i):
        span = pl.ds(i * piece, piece)
        return pltpu.make_async_remote_copy(
            src_ref=q_out.at[s, t, span], dst_ref=q_in.at[s + 1, t, span],
            send_sem=ring_send.at[s, t, i], recv_sem=ring_recv.at[s + 1, t, i],
            device_id=after if t == 0 else before, device_id_type=MESH,
        )

    def ring_arrival(s, t, i):
        span = pl.ds(i * piece, piece)
        return pltpu.make_async_remote_copy(
            src_ref=q_out.at[s, t, span], dst_ref=q_in.at[s, t, span],
            send_sem=ring_send.at[s, t, i], recv_sem=ring_recv.at[s, t, i],
            device_id=after if t == 0 else before, device_id_type=MESH,
        )

    own = z * TABLES + c

    def mate_copy(p):
        return pltpu.make_async_remote_copy(
            src_ref=q_out.at[mid - 1, TABLES - 1 - c, pl.ds(p * rows, rows)],
            dst_ref=gath[p].at[own],
            send_sem=core_send.at[p], recv_sem=core_recv.at[p],
            device_id=mate, device_id_type=MESH,
        )

    def lead_copy(p, way, src):
        slot = gath[p].at[pl.ds(src * TABLES + c, 1)]
        return pltpu.make_async_remote_copy(
            src_ref=slot, dst_ref=slot,
            send_sem=lead_send.at[p, way], recv_sem=lead_recv.at[p, way],
            device_id=up if way == 0 else down, device_id_type=MESH,
        )

    def line_slot(p, k, src):
        if k == 0:
            return gath[p].at[pl.ds(src * TABLES + (TABLES - 1 - c), 1)]
        return gath[p].at[pl.ds(src * TABLES, TABLES)]

    def line_copy(p, k, way):
        slot = line_slot(p, k, z - k if way == 0 else z + k)
        return pltpu.make_async_remote_copy(
            src_ref=slot, dst_ref=slot,
            send_sem=line_send.at[p, k, way], recv_sem=line_recv.at[p, k, way],
            device_id=up if way == 0 else down, device_id_type=MESH,
        )

    def line_sends(k, way):
        if way == 0:
            return jnp.logical_and(z - k >= 0, z + 1 < line)
        return jnp.logical_and(z + k < line, z > 0)

    def line_arrival(p, k, way):
        slot = line_slot(p, k, z - k - 1 if way == 0 else z + k + 1)
        return pltpu.make_async_remote_copy(
            src_ref=slot, dst_ref=slot,
            send_sem=line_send.at[p, k, way], recv_sem=line_recv.at[p, k, way],
            device_id=up if way == 0 else down, device_id_type=MESH,
        )

    def line_gets(k, way):
        return z - k - 1 >= 0 if way == 0 else z + k + 1 < line

    chips = pairs * inner
    chip = y * inner + x

    def all_copy(p, i):
        return pltpu.make_async_remote_copy(
            src_ref=outb[p].at[i], dst_ref=fin[p].at[c * chips + chip],
            send_sem=all_send.at[p, i], recv_sem=all_recv.at[p, i],
            device_id=peer(*offsets[i]), device_id_type=MESH,
        )

    def all_arrival(p, i):
        dy, dx, dc = offsets[i]
        source = lax.rem(y + pairs - dy, pairs) * inner + lax.rem(x + inner - dx, inner)
        return pltpu.make_async_remote_copy(
            src_ref=outb[p].at[i],
            dst_ref=fin[p].at[lax.rem(c + TABLES - dc, TABLES) * chips + source],
            send_sem=all_send.at[p, i], recv_sem=all_recv.at[p, i],
            device_id=peer(*offsets[i]), device_id_type=MESH,
        )

    def exchange_start():
        for p in range(PARTS):
            mate_copy(p).start()
            gath[p][own] = q_out[mid - 1, c, pl.ds(p * rows, rows)]
            for way in range(2):
                @pl.when(line_sends(0, way))
                def _():
                    lead_copy(p, way, z).start()

    def exchange():
        step = jnp.where(c == 0, 1, count - 1)
        holders = []
        for zs in range(line):
            for cs in range(TABLES):
                src = (y * TABLES + cs) * columns + zs * inner + x
                holders.append(owners[c, lax.rem(src + step, count)])

        def pick(device):
            target = device[0] * columns + device[1]
            j = jnp.int32(0)
            for k, holder in enumerate(holders):
                j = jnp.where(holder == target, k, j)
            return j

        picks = [pick(peer(*o)) for o in offsets]
        self_pick = pick((g, b))
        origin = []
        for t in range(TABLES):
            found = jnp.int32(0)
            for src in range(count):
                sg, sb = divmod(src, columns)
                shifted = (src + (1 if t == 0 else count - 1)) % count
                found = jnp.where(
                    owners[t, shifted] == me, (sg // TABLES) * inner + sb % inner, found
                )
            origin.append(t * chips + found)

        def advance(p, k):
            if k == 0:
                arrived = pltpu.make_async_remote_copy(
                    src_ref=q_out.at[mid - 1, TABLES - 1 - c, pl.ds(p * rows, rows)],
                    dst_ref=gath[p].at[z * TABLES + (TABLES - 1 - c)],
                    send_sem=core_send.at[p], recv_sem=core_recv.at[p],
                    device_id=mate, device_id_type=MESH,
                )
                arrived.wait_recv()
            else:
                for way in range(2):
                    @pl.when(line_gets(k - 1, way))
                    def _():
                        if k == 1:
                            lead_copy(p, way, z - 1 if way == 0 else z + 1).wait_recv()
                        line_arrival(p, k - 1, way).wait_recv()
            if k < line - 1:
                for way in range(2):
                    @pl.when(line_sends(k, way))
                    def _():
                        line_copy(p, k, way).start()
            else:
                for i in range(len(offsets)):
                    outb[p][i] = gath[p][picks[i]]
                    all_copy(p, i).start()
                fin[p][c * chips + chip] = gath[p][self_pick]

        for wave in range(PARTS + line - 1):
            for p in range(PARTS):
                if 0 <= wave - p < line:
                    advance(p, wave - p)
        for p in range(PARTS):
            for i in range(len(offsets)):
                all_arrival(p, i).wait_recv()
            for t in range(TABLES):
                q_in[mid, t, pl.ds(p * rows, rows)] = fin[p][origin[t]]
        for p in range(PARTS):
            mate_copy(p).wait_send()
            for k in range(line - 1):
                for way in range(2):
                    @pl.when(line_sends(k, way))
                    def _():
                        if k == 0:
                            lead_copy(p, way, z).wait_send()
                        line_copy(p, k, way).wait_send()
            for i in range(len(offsets)):
                all_copy(p, i).wait_send()

    pieces = [(i, t) for i in range(SPLIT) for t in range(TABLES)]

    def stratum(s, carry):
        load_rate(s).wait()
        load_mask(s).wait()

        @pl.when(s + early < strata)
        def _():
            issue(s + early)

        for k, (i, t) in enumerate(pieces):
            @pl.when(jnp.logical_and(s > 0, s != mid))
            def _():
                ring_arrival(s, t, i).wait_recv()

            span = slice(i * piece, (i + 1) * piece)
            part = slice(t * half + i * piece, t * half + (i + 1) * piece)
            block = q_in[s, t, span]
            pred = lax.dot_general(
                user_b[...], block, (((1,), (1,)), ((), ())),
                preferred_element_type=jnp.float32,
            )
            err[:, part] = jnp.where(
                mask_buf[s, :, part] == 1,
                pred - rate_buf[s, :, part].astype(jnp.float32), 0.0,
            ).astype(jnp.bfloat16)
            grad_item = lax.dot_general(
                err[:, part], user_b[...], (((0,), (0,)), ((), ())),
                preferred_element_type=jnp.float32,
            )
            block_f = block.astype(jnp.float32)
            q_out[s, t, span] = (
                block_f - RATE * (grad_item + DECAY * block_f)
            ).astype(jnp.bfloat16)

            if k == 0:
                @pl.when(s == 0)
                def _():
                    pl.semaphore_wait(barrier, greeted)

            @pl.when(jnp.logical_and(s < strata - 1, s != mid - 1))
            def _():
                ring(s, t, i).start()

            if k == len(pieces) - 1:
                @pl.when(s == mid - 1)
                def _():
                    exchange_start()

            grad_user = jnp.dot(err[:, part], block, preferred_element_type=jnp.float32)
            if k == 0:
                total[...] = grad_user
            elif k < len(pieces) - 1:
                total[...] += grad_user
            else:
                old = users[...]
                new = old - RATE * (total[...] + grad_user + DECAY * old)
                users[...] = new
                user_b[...] = new.astype(jnp.bfloat16)

        @pl.when(s == mid - 1)
        def _():
            exchange()

        return carry

    lax.fori_loop(0, strata, stratum, 0)
    ahead_out[...] = q_out[strata - 1, 0]
    behind_out[...] = q_out[strata - 1, 1]

    def drain(s, carry):
        @pl.when(s != mid - 1)
        def _():
            for i, t in pieces:
                ring(s, t, i).wait_send()
        return carry

    lax.fori_loop(0, strata - 1, drain, 0)


def settle(arrays):
    shapes = tuple(jax.ShapeDtypeStruct(a.shape, a.dtype) for a in arrays)
    n = len(arrays)
    where = pl.BlockSpec(memory_space=pltpu.VMEM)

    def copies(*refs):
        for i in range(n):
            refs[n + i][...] = refs[i][...]

    return pl.pallas_call(
        copies, out_shape=shapes, in_specs=[where] * n, out_specs=(where,) * n,
    )(*arrays)


def body(ratings, rated, user_factors, item_ahead, item_behind, owners):
    groups = lax.axis_size("grp")
    columns = lax.axis_size("blk")
    strata, own_users, items = ratings.shape
    half, rank = item_ahead.shape
    rows = half // PARTS
    line, inner = line_split(columns)
    chips = (groups // TABLES) * inner
    peers = chips * TABLES - 1
    vmem = pl.BlockSpec(memory_space=pltpu.VMEM)
    anywhere = pl.BlockSpec(memory_space=pl.ANY)
    bf16 = jnp.bfloat16
    dma = pltpu.SemaphoreType.DMA
    scratch = (
        [
            pltpu.VMEM((strata, own_users, items), ratings.dtype),
            pltpu.VMEM((strata, own_users, items), rated.dtype),
            pltpu.VMEM((strata, TABLES, half, rank), bf16),
            pltpu.VMEM((strata, TABLES, half, rank), bf16),
            pltpu.VMEM((own_users, rank), bf16),
            pltpu.VMEM((own_users, items), bf16),
            pltpu.VMEM((own_users, rank), jnp.float32),
        ]
        + [pltpu.VMEM((line * TABLES, rows, rank), bf16)] * PARTS
        + [pltpu.VMEM((peers, rows, rank), bf16)] * PARTS
        + [pltpu.VMEM((TABLES * chips, rows, rank), bf16)] * PARTS
        + [
            dma((strata,)), dma((strata,)),
            dma((strata, TABLES, SPLIT)), dma((strata, TABLES, SPLIT)),
            dma((PARTS,)), dma((PARTS,)),
            dma((PARTS, line - 1, 2)), dma((PARTS, line - 1, 2)),
            dma((PARTS, 2)), dma((PARTS, 2)),
            dma((PARTS, peers)), dma((PARTS, peers)),
        ]
    )
    moved = pl.pallas_call(
        functools.partial(kernel, groups, columns, strata),
        out_shape=(
            jax.ShapeDtypeStruct(user_factors.shape, jnp.float32),
            jax.ShapeDtypeStruct(item_ahead.shape, bf16),
            jax.ShapeDtypeStruct(item_behind.shape, bf16),
        ),
        in_specs=[anywhere, anywhere, vmem, vmem, vmem,
                  pl.BlockSpec(memory_space=pltpu.SMEM)],
        out_specs=(vmem, vmem, vmem),
        scratch_shapes=scratch,
        compiler_params=pltpu.CompilerParams(
            collective_id=0, has_side_effects=True, vmem_limit_bytes=56 * 1024 * 1024
        ),
        cost_estimate=pl.CostEstimate(
            flops=6 * strata * own_users * items * rank,
            bytes_accessed=6 * strata * own_users * items, transcendentals=0,
        ),
    )(ratings, rated, user_factors, item_ahead, item_behind, owners)
    return settle(moved)


def solution(mesh):
    shard = P(("grp", "blk"), None)
    strata = P(None, ("grp", "blk"), None)
    return jax.shard_map(
        body, mesh=mesh,
        in_specs=(strata, strata, shard, shard, shard, P()),
        out_specs=(shard, shard, shard), check_vma=False,
    )
```

```python
import functools

import jax
import jax.numpy as jnp
from jax import lax
from jax.experimental import pallas as pl
from jax.experimental.pallas import tpu as pltpu
from jax.sharding import PartitionSpec as P

RATE = 0.005
DECAY = 0.05
TABLES = 2
AHEAD = 2
SPLIT = 2
PARTS = 2
MESH = pl.DeviceIdType.MESH


def line_split(columns):
    inner = 1
    while columns % (inner * inner * 4) == 0 or (columns % (inner * 2) == 0 and inner * inner * 4 <= columns):
        inner *= 2
    return columns // inner, inner


def kernel(
    groups, columns, strata,
    ratings, rated, users_in, ahead_in, behind_in, owners,
    users, ahead_out, behind_out,
    rate_buf, mask_buf, q_in, q_out, user_b, err, total,
    *rest,
):
    gath = rest[:PARTS]
    outb = rest[PARTS:2 * PARTS]
    fin = rest[2 * PARTS:3 * PARTS]
    (rate_sem, mask_sem, ring_send, ring_recv, core_send, core_recv,
     line_send, line_recv, lead_send, lead_recv, all_send, all_recv) = rest[3 * PARTS:]

    count = groups * columns
    line, inner = line_split(columns)
    pairs = groups // TABLES
    mid = strata // 2
    half = ahead_in.shape[0]
    rows = half // PARTS

    g = lax.axis_index("grp")
    b = lax.axis_index("blk")
    me = g * columns + b
    c = lax.rem(g, TABLES)
    y = lax.div(g, TABLES)
    z = lax.div(b, inner)
    x = lax.rem(b, inner)

    def load_rate(s):
        return pltpu.make_async_copy(ratings.at[s], rate_buf.at[s], rate_sem.at[s])

    def load_mask(s):
        return pltpu.make_async_copy(rated.at[s], mask_buf.at[s], mask_sem.at[s])

    def at(d):
        return (lax.div(d, columns), lax.rem(d, columns))

    after = at(lax.rem(me + 1, count))
    before = at(lax.rem(me + count - 1, count))
    mate = (y * TABLES + (TABLES - 1 - c), b)
    up = (g, jnp.minimum(z + 1, line - 1) * inner + x)
    down = (g, jnp.maximum(z - 1, 0) * inner + x)
    offsets = [
        (dy, dx, dc)
        for dy in range(pairs) for dx in range(inner) for dc in range(TABLES)
        if (dy, dx, dc) != (0, 0, 0)
    ]

    def peer(dy, dx, dc):
        return (
            lax.rem(y + dy, pairs) * TABLES + lax.rem(c + dc, TABLES),
            z * inner + lax.rem(x + dx, inner),
        )

    barrier = pltpu.get_barrier_semaphore()

    def greet(device):
        pl.semaphore_signal(barrier, inc=1, device_id=device, device_id_type=MESH)

    greet(after)
    greet(before)
    for o in offsets:
        greet(peer(*o))

    @pl.when(z + 1 < line)
    def _():
        greet(up)

    @pl.when(z > 0)
    def _():
        greet(down)

    def issue(s):
        load_rate(s).start()
        load_mask(s).start()

    early = min(AHEAD, strata)
    for s in range(early):
        issue(s)

    q_in[0, 0] = ahead_in[...]
    q_in[0, 1] = behind_in[...]
    users[...] = users_in[...]
    user_b[...] = users_in[...].astype(jnp.bfloat16)

    greeted = 2 + len(offsets)
    greeted = greeted + jnp.where(z + 1 < line, 1, 0) + jnp.where(z > 0, 1, 0)

    piece = half // SPLIT

    def ring(s, t, i):
        span = pl.ds(i * piece, piece)
        return pltpu.make_async_remote_copy(
            src_ref=q_out.at[s, t, span], dst_ref=q_in.at[s + 1, t, span],
            send_sem=ring_send.at[s, t, i], recv_sem=ring_recv.at[s + 1, t, i],
            device_id=after if t == 0 else before, device_id_type=MESH,
        )

    def ring_arrival(s, t, i):
        span = pl.ds(i * piece, piece)
        return pltpu.make_async_remote_copy(
            src_ref=q_out.at[s, t, span], dst_ref=q_in.at[s, t, span],
            send_sem=ring_send.at[s, t, i], recv_sem=ring_recv.at[s, t, i],
            device_id=after if t == 0 else before, device_id_type=MESH,
        )

    own = z * TABLES + c

    def mate_copy(p):
        return pltpu.make_async_remote_copy(
            src_ref=q_out.at[mid - 1, TABLES - 1 - c, pl.ds(p * rows, rows)],
            dst_ref=gath[p].at[own],
            send_sem=core_send.at[p], recv_sem=core_recv.at[p],
            device_id=mate, device_id_type=MESH,
        )

    def lead_copy(p, way, src):
        slot = gath[p].at[pl.ds(src * TABLES + c, 1)]
        return pltpu.make_async_remote_copy(
            src_ref=slot, dst_ref=slot,
            send_sem=lead_send.at[p, way], recv_sem=lead_recv.at[p, way],
            device_id=up if way == 0 else down, device_id_type=MESH,
        )

    def line_slot(p, k, src):
        if k == 0:
            return gath[p].at[pl.ds(src * TABLES + (TABLES - 1 - c), 1)]
        return gath[p].at[pl.ds(src * TABLES, TABLES)]

    def line_copy(p, k, way):
        slot = line_slot(p, k, z - k if way == 0 else z + k)
        return pltpu.make_async_remote_copy(
            src_ref=slot, dst_ref=slot,
            send_sem=line_send.at[p, k, way], recv_sem=line_recv.at[p, k, way],
            device_id=up if way == 0 else down, device_id_type=MESH,
        )

    def line_sends(k, way):
        if way == 0:
            return jnp.logical_and(z - k >= 0, z + 1 < line)
        return jnp.logical_and(z + k < line, z > 0)

    def line_arrival(p, k, way):
        slot = line_slot(p, k, z - k - 1 if way == 0 else z + k + 1)
        return pltpu.make_async_remote_copy(
            src_ref=slot, dst_ref=slot,
            send_sem=line_send.at[p, k, way], recv_sem=line_recv.at[p, k, way],
            device_id=up if way == 0 else down, device_id_type=MESH,
        )

    def line_gets(k, way):
        return z - k - 1 >= 0 if way == 0 else z + k + 1 < line

    chips = pairs * inner
    chip = y * inner + x

    def all_copy(p, i):
        return pltpu.make_async_remote_copy(
            src_ref=outb[p].at[i], dst_ref=fin[p].at[c * chips + chip],
            send_sem=all_send.at[p, i], recv_sem=all_recv.at[p, i],
            device_id=peer(*offsets[i]), device_id_type=MESH,
        )

    def all_arrival(p, i):
        dy, dx, dc = offsets[i]
        source = lax.rem(y + pairs - dy, pairs) * inner + lax.rem(x + inner - dx, inner)
        return pltpu.make_async_remote_copy(
            src_ref=outb[p].at[i],
            dst_ref=fin[p].at[lax.rem(c + TABLES - dc, TABLES) * chips + source],
            send_sem=all_send.at[p, i], recv_sem=all_recv.at[p, i],
            device_id=peer(*offsets[i]), device_id_type=MESH,
        )

    origin = []
    for t in range(TABLES):
        found = jnp.int32(0)
        for src in range(count):
            sg, sb = divmod(src, columns)
            shifted = (src + (1 if t == 0 else count - 1)) % count
            found = jnp.where(
                owners[t, shifted] == me, (sg // TABLES) * inner + sb % inner, found
            )
        origin.append(t * chips + found)

    def collect(i_piece):
        for p in range(PARTS):
            if p * SPLIT // PARTS != i_piece:
                continue
            for i in range(len(offsets)):
                all_arrival(p, i).wait_recv()
            for t in range(TABLES):
                q_in[mid, t, pl.ds(p * rows, rows)] = fin[p][origin[t]]

    def exchange_start():
        for p in range(PARTS):
            mate_copy(p).start()
            gath[p][own] = q_out[mid - 1, c, pl.ds(p * rows, rows)]
            for way in range(2):
                @pl.when(line_sends(0, way))
                def _():
                    lead_copy(p, way, z).start()

    def exchange():
        step = jnp.where(c == 0, 1, count - 1)
        holders = []
        for zs in range(line):
            for cs in range(TABLES):
                src = (y * TABLES + cs) * columns + zs * inner + x
                holders.append(owners[c, lax.rem(src + step, count)])

        def pick(device):
            target = device[0] * columns + device[1]
            j = jnp.int32(0)
            for k, holder in enumerate(holders):
                j = jnp.where(holder == target, k, j)
            return j

        picks = [pick(peer(*o)) for o in offsets]
        self_pick = pick((g, b))
        def advance(p, k):
            if k == 0:
                arrived = pltpu.make_async_remote_copy(
                    src_ref=q_out.at[mid - 1, TABLES - 1 - c, pl.ds(p * rows, rows)],
                    dst_ref=gath[p].at[z * TABLES + (TABLES - 1 - c)],
                    send_sem=core_send.at[p], recv_sem=core_recv.at[p],
                    device_id=mate, device_id_type=MESH,
                )
                arrived.wait_recv()
            else:
                for way in range(2):
                    @pl.when(line_gets(k - 1, way))
                    def _():
                        if k == 1:
                            lead_copy(p, way, z - 1 if way == 0 else z + 1).wait_recv()
                        line_arrival(p, k - 1, way).wait_recv()
            if k < line - 1:
                for way in range(2):
                    @pl.when(line_sends(k, way))
                    def _():
                        line_copy(p, k, way).start()
            else:
                for i in range(len(offsets)):
                    outb[p][i] = gath[p][picks[i]]
                    all_copy(p, i).start()
                fin[p][c * chips + chip] = gath[p][self_pick]

        for wave in range(PARTS + line - 1):
            for p in range(PARTS):
                if 0 <= wave - p < line:
                    advance(p, wave - p)
    def exchange_drain():
        for p in range(PARTS):
            mate_copy(p).wait_send()
            for k in range(line - 1):
                for way in range(2):
                    @pl.when(line_sends(k, way))
                    def _():
                        if k == 0:
                            lead_copy(p, way, z).wait_send()
                        line_copy(p, k, way).wait_send()
            for i in range(len(offsets)):
                all_copy(p, i).wait_send()

    pieces = [(i, t) for i in range(SPLIT) for t in range(TABLES)]

    def stratum(s, carry):
        load_rate(s).wait()
        load_mask(s).wait()

        @pl.when(s + early < strata)
        def _():
            issue(s + early)

        for k, (i, t) in enumerate(pieces):
            @pl.when(jnp.logical_and(s > 0, s != mid))
            def _():
                ring_arrival(s, t, i).wait_recv()

            if t == 0:
                @pl.when(s == mid)
                def _():
                    collect(i)

            span = slice(i * piece, (i + 1) * piece)
            part = slice(t * half + i * piece, t * half + (i + 1) * piece)
            block = q_in[s, t, span]
            pred = lax.dot_general(
                user_b[...], block, (((1,), (1,)), ((), ())),
                preferred_element_type=jnp.float32,
            )
            err[:, part] = jnp.where(
                mask_buf[s, :, part] == 1,
                pred - rate_buf[s, :, part].astype(jnp.float32), 0.0,
            ).astype(jnp.bfloat16)
            grad_item = lax.dot_general(
                err[:, part], user_b[...], (((0,), (0,)), ((), ())),
                preferred_element_type=jnp.float32,
            )
            block_f = block.astype(jnp.float32)
            q_out[s, t, span] = (
                block_f - RATE * (grad_item + DECAY * block_f)
            ).astype(jnp.bfloat16)

            if k == 0:
                @pl.when(s == 0)
                def _():
                    pl.semaphore_wait(barrier, greeted)

            @pl.when(jnp.logical_and(s < strata - 1, s != mid - 1))
            def _():
                ring(s, t, i).start()

            if k == len(pieces) - 1:
                @pl.when(s == mid - 1)
                def _():
                    exchange_start()

            grad_user = jnp.dot(err[:, part], block, preferred_element_type=jnp.float32)
            if k == 0:
                total[...] = grad_user
            elif k < len(pieces) - 1:
                total[...] += grad_user
            else:
                old = users[...]
                new = old - RATE * (total[...] + grad_user + DECAY * old)
                users[...] = new
                user_b[...] = new.astype(jnp.bfloat16)

        @pl.when(s == mid - 1)
        def _():
            exchange()

        return carry

    lax.fori_loop(0, strata, stratum, 0)
    ahead_out[...] = q_out[strata - 1, 0]
    behind_out[...] = q_out[strata - 1, 1]

    def drain(s, carry):
        @pl.when(s != mid - 1)
        def _():
            for i, t in pieces:
                ring(s, t, i).wait_send()
        return carry

    lax.fori_loop(0, strata - 1, drain, 0)
    exchange_drain()


def settle(arrays):
    shapes = tuple(jax.ShapeDtypeStruct(a.shape, a.dtype) for a in arrays)
    n = len(arrays)
    where = pl.BlockSpec(memory_space=pltpu.VMEM)

    def copies(*refs):
        for i in range(n):
            refs[n + i][...] = refs[i][...]

    return pl.pallas_call(
        copies, out_shape=shapes, in_specs=[where] * n, out_specs=(where,) * n,
    )(*arrays)


def body(ratings, rated, user_factors, item_ahead, item_behind, owners):
    groups = lax.axis_size("grp")
    columns = lax.axis_size("blk")
    strata, own_users, items = ratings.shape
    half, rank = item_ahead.shape
    rows = half // PARTS
    line, inner = line_split(columns)
    chips = (groups // TABLES) * inner
    peers = chips * TABLES - 1
    vmem = pl.BlockSpec(memory_space=pltpu.VMEM)
    anywhere = pl.BlockSpec(memory_space=pl.ANY)
    bf16 = jnp.bfloat16
    dma = pltpu.SemaphoreType.DMA
    scratch = (
        [
            pltpu.VMEM((strata, own_users, items), ratings.dtype),
            pltpu.VMEM((strata, own_users, items), rated.dtype),
            pltpu.VMEM((strata, TABLES, half, rank), bf16),
            pltpu.VMEM((strata, TABLES, half, rank), bf16),
            pltpu.VMEM((own_users, rank), bf16),
            pltpu.VMEM((own_users, items), bf16),
            pltpu.VMEM((own_users, rank), jnp.float32),
        ]
        + [pltpu.VMEM((line * TABLES, rows, rank), bf16)] * PARTS
        + [pltpu.VMEM((peers, rows, rank), bf16)] * PARTS
        + [pltpu.VMEM((TABLES * chips, rows, rank), bf16)] * PARTS
        + [
            dma((strata,)), dma((strata,)),
            dma((strata, TABLES, SPLIT)), dma((strata, TABLES, SPLIT)),
            dma((PARTS,)), dma((PARTS,)),
            dma((PARTS, line - 1, 2)), dma((PARTS, line - 1, 2)),
            dma((PARTS, 2)), dma((PARTS, 2)),
            dma((PARTS, peers)), dma((PARTS, peers)),
        ]
    )
    moved = pl.pallas_call(
        functools.partial(kernel, groups, columns, strata),
        out_shape=(
            jax.ShapeDtypeStruct(user_factors.shape, jnp.float32),
            jax.ShapeDtypeStruct(item_ahead.shape, bf16),
            jax.ShapeDtypeStruct(item_behind.shape, bf16),
        ),
        in_specs=[anywhere, anywhere, vmem, vmem, vmem,
                  pl.BlockSpec(memory_space=pltpu.SMEM)],
        out_specs=(vmem, vmem, vmem),
        scratch_shapes=scratch,
        compiler_params=pltpu.CompilerParams(
            collective_id=0, has_side_effects=True, vmem_limit_bytes=56 * 1024 * 1024
        ),
        cost_estimate=pl.CostEstimate(
            flops=6 * strata * own_users * items * rank,
            bytes_accessed=6 * strata * own_users * items, transcendentals=0,
        ),
    )(ratings, rated, user_factors, item_ahead, item_behind, owners)
    return settle(moved)


def solution(mesh):
    shard = P(("grp", "blk"), None)
    strata = P(None, ("grp", "blk"), None)
    return jax.shard_map(
        body, mesh=mesh,
        in_specs=(strata, strata, shard, shard, shard, P()),
        out_specs=(shard, shard, shard), check_vma=False,
    )
```
